32 devices in a mesh: grp: 4 (over y, x), mem: 8 (over z, core).
Axes of the slice: x: 2, y: 2, z: 4, core: 2. Of those that a mesh axis runs over, the one named last changes fastest.
Arguments:
- embedding: bfloat16 [32768, 768], P(('grp', 'mem')), parts along dimension 0, may hold values from -127 to 127, as said below
- row_scale: float32 [32768], P(('grp', 'mem')), parts along dimension 0, may hold values from 0.0004 to 0.0006
- block_rows: int32 [64], P(('grp', 'mem')), parts along dimension 0, may hold values from 1 to 512, 6144 in all
- requests: int32 [32, 8], P(('grp', 'mem')), parts along dimension 0, may hold values from 0 to 1
Outputs:
- highest: float32 [32768], P(('grp', 'mem')), parts along dimension 0
The draws below stay inside these ranges and needn't reach their ends.
There are 4 independent parts, one for each index of `grp`. The reference program is written for one: setup_inputs(seed, part) draws one part's arguments, and reference() takes and returns one part's arrays. A program takes and returns all parts, laid end to end along the dimension named above; each array names one. Nothing has to cross between parts.
Inputs may be any that keep to these rules, and one draw needn't show every extreme that they name: `embedding`: whole numbers, held exactly. `block_rows`: the largest block holds exactly 512 live rows.
All inputs are finite; a program needn't handle non-finite values.
Results may differ from the reference program's by a relative error of at most 0.0012.
Values may be sent and summed in bfloat16 or wider, within the bound.
A program may use at most 128 MiB of HBM per device.

```python
import math
import jax
import jax.numpy as jnp
import numpy as np
from jax import lax

D = 768
BLOCK = 512
BLK_DEV = 2
NBLK = 16
ROWS = 8192
N_MEM = 8


def draw_embedding(key, part):
    key = jax.random.fold_in(key, 11)
    first = jax.random.fold_in(key, 0)
    codes = jax.random.randint(first, (ROWS, D), -127, 128, dtype=jnp.int32)
    return codes.astype(jnp.bfloat16)


def set_ends(values, stream_key, smallest, high):
    longest = values.shape.index(max(values.shape))
    spots = []
    for shift in (0, 1):
        where = [jax.random.randint(jax.random.fold_in(stream_key, axis), (), 0, length) for axis, length in enumerate(values.shape)]
        where[longest] = (where[longest] + shift) % values.shape[longest]
        spots.append(tuple(where))
    return values.at[spots[0]].set(smallest).at[spots[1]].set(high)


def block_levels(stream_key, shape, pieces, smallest, largest):
    gain, own = 1.0, jax.random.fold_in(stream_key, 6)
    for axis_at, blocks in pieces:
        heights = jnp.exp(jax.random.uniform(jax.random.fold_in(own, axis_at), (blocks,), jnp.float32, smallest / len(pieces), largest / len(pieces)))
        gain = gain * jnp.repeat(heights, shape[axis_at] // blocks).reshape([-1 if axis == axis_at else 1 for axis in range(len(shape))])
    return gain


def length_profile(amount, total, bound, lean):
    loads = [(1 << 20) // math.isqrt(standing ** lean) + 1 for standing in range(2, amount + 1)]
    spare, holding = total - bound - (amount - 1), [1] * (amount - 1)
    while spare > 0:
        free = [i for i in range(amount - 1) if holding[i] < bound]
        mass, budget = sum([loads[i] for i in free]), spare
        for i in free:
            extra = min(bound - holding[i], max(1, budget * loads[i] // mass), spare)
            holding[i] = holding[i] + extra
            spare = spare - extra
    return np.array([bound] + holding)


def ragged(stream_key, number_of, total, limit, skew):
    if number_of == 2:
        one = jax.random.randint(stream_key, (), max(1, total - limit), min(limit, total - 1) + 1)
        return jnp.stack([one, total - one])
    sizes = jnp.asarray(length_profile(number_of, total, limit, skew), jnp.int32)
    pairs = (number_of - 1) // 2
    source_of, sink = sizes[1:1 + 2 * pairs:2], sizes[2:2 + 2 * pairs:2]
    margin = jnp.minimum(source_of - 1, limit - sink)
    shifted = jax.random.randint(jax.random.fold_in(stream_key, 1), (pairs,), 0, 1 << 20) % (margin + 1)
    sizes = sizes.at[1:1 + 2 * pairs:2].set(source_of - shifted).at[2:2 + 2 * pairs:2].set(sink + shifted)
    return sizes[jax.random.permutation(jax.random.fold_in(stream_key, 2), number_of)]


def setup_inputs(seed: int = 0, part: int = 0) -> dict:
    arg_keys = jax.random.split(jax.random.key(seed), 5)
    own_keys = jax.random.split(jax.random.fold_in(arg_keys[4], part), 5)
    embedding = draw_embedding(jax.random.fold_in(jax.random.fold_in(arg_keys[4], part), 71), part)
    row_scale = jnp.clip(jnp.exp(math.log(0.0006) - 0.4054652 * jax.random.uniform(own_keys[1], (ROWS,), jnp.float32) ** block_levels(own_keys[1], (ROWS,), ((0, 8),), -0.2, 0.2)), 0.0004, 0.0006)
    block_rows = ragged(own_keys[2], NBLK, NBLK * BLOCK * 3 // 4, BLOCK, 2).astype(jnp.int32)
    requests = set_ends(jax.random.randint(own_keys[3], (N_MEM, N_MEM), 0, BLK_DEV), jax.random.fold_in(own_keys[3], 1), 0, BLK_DEV - 1).astype(jnp.int32)
    return dict(embedding=embedding, row_scale=row_scale, block_rows=block_rows, requests=requests)


def reference(embedding, row_scale, block_rows, requests):
    blocks_all = block_rows.shape[0]
    per_device = blocks_all // N_MEM
    decoded = (embedding.astype(jnp.float32) * row_scale[:, None]).astype(jnp.bfloat16)
    decoded = decoded.reshape(blocks_all, BLOCK, decoded.shape[1])
    positions = jnp.arange(BLOCK, dtype=jnp.int32)
    live = positions[None, :] < block_rows[:, None]
    asker = jnp.arange(N_MEM, dtype=jnp.int32)[:, None, None]
    owner = jnp.arange(N_MEM, dtype=jnp.int32)[None, :, None]
    local = jnp.arange(per_device, dtype=jnp.int32)[None, None, :]
    shape = (N_MEM, N_MEM, per_device)
    left_block = jnp.broadcast_to(asker * per_device + local, shape).reshape(-1).astype(jnp.int32)
    right_block = jnp.broadcast_to(owner * per_device + requests[:, :, None], shape).reshape(-1).astype(jnp.int32)
    identity = positions[:, None] == positions[None, :]

    def visit(running, entries):
        left, right = entries
        scores = jnp.dot(decoded[left], decoded[right].T, preferred_element_type=jnp.float32)
        allowed = live[right][None, :] & jnp.logical_not(identity & (left == right))
        masked = jnp.where(allowed, scores, jnp.float32(-1e30))
        running = running.at[left].max(jnp.max(masked, axis=1))
        column = jnp.max(jnp.where(live[left][:, None], masked, jnp.float32(-1e30)), axis=0)
        running = running.at[right].max(column)
        return running, None

    start = jnp.full((blocks_all, BLOCK), -1e30, dtype=jnp.float32)
    highest, _ = lax.scan(visit, start, (left_block, right_block))
    return jnp.where(live, highest, jnp.float32(0.0)).reshape(-1)
```

```python
import jax
import jax.numpy as jnp
from jax import lax
from jax.experimental import pallas as pl
from jax.experimental.pallas import tpu as pltpu
from jax.sharding import PartitionSpec as P

BLOCK = 512
CHUNK = 64
AHEAD = 4
LOW = -1e30
MESH = pl.DeviceIdType.MESH


def shards(embedding, row_scale, block_rows, requests):
    members = lax.axis_size("mem")
    myself = lax.axis_index("mem")
    blocks_here = block_rows.shape[0]
    width = embedding.shape[1]
    decoded = (embedding.astype(jnp.float32) * row_scale[:, None]).astype(jnp.bfloat16)
    decoded = decoded.reshape(blocks_here, BLOCK, width)
    positions = jnp.arange(BLOCK, dtype=jnp.int32)
    local_live = positions[None, :] < block_rows[:, None]
    all_rows = lax.all_gather(block_rows, "mem", axis=0, tiled=True)
    wanted = lax.all_to_all(requests, "mem", split_axis=1, concat_axis=0, tiled=True)[:, 0]
    chosen = requests[0]
    local_ids = jnp.arange(blocks_here, dtype=jnp.int32)
    identity = positions[:, None] == positions[None, :]
    row_init = jnp.full((blocks_here, BLOCK), -1e30, dtype=jnp.float32)
    outgoing = jnp.take(decoded, wanted, axis=0)
    fetched = lax.all_to_all(outgoing, "mem", split_axis=0, concat_axis=0, tiled=True)
    owners = jnp.arange(members, dtype=jnp.int32)
    columns_live = positions[None, :] < all_rows[owners * blocks_here + chosen][:, None]
    own_block = jnp.where(owners == myself, chosen, -1)

    def visit(running, entries):
        partner, columns, own_index = entries
        scores = jnp.einsum("arc,sc->ars", decoded, partner, preferred_element_type=jnp.float32)
        diagonal = (local_ids[:, None, None] == own_index) & identity[None, :, :]
        allowed = columns[None, None, :] & jnp.logical_not(diagonal)
        masked = jnp.where(allowed, scores, jnp.float32(-1e30))
        running = jnp.maximum(running, jnp.max(masked, axis=2))
        column = jnp.max(jnp.where(local_live[:, :, None], masked, jnp.float32(-1e30)), axis=(0, 1))
        return (running, column)

    row_best, col_best = lax.scan(visit, row_init, (fetched, columns_live, own_block))
    returned = lax.all_to_all(col_best, "mem", split_axis=0, concat_axis=0, tiled=True)
    matches = wanted[None, :, None] == local_ids[:, None, None]
    incoming = jnp.max(jnp.where(matches, returned[None, :, :], jnp.float32(-1e30)), axis=1)
    highest = jnp.maximum(row_best, incoming)
    return jnp.where(local_live, highest, jnp.float32(0.0)).reshape(-1)


def scores_of(x, y):
    return lax.dot_general(x, y, (((1,), (1,)), ((), ())), preferred_element_type=jnp.float32)


def kernel(
    rows_ref, own_ref, req_ref, out_ref,
    chip, held, passing, other, best, out_x, out_y, reqs,
    own_send, own_send2, held_send, passing_send, other_send, sib_send,
    held_recv, passing_recv, other_recv, sib_recv, chip_sems,
    best_recv, x_send, y_send, req_send, req_recv,
):
    grp, me = lax.axis_index("grp"), lax.axis_index("mem")
    core, z = me % 2, me // 2
    side = grp % 2
    w = z + side * (3 - 2 * z)
    pgrp = grp + 1 - 2 * side
    sib = me + 1 - 2 * core
    n_chunks = own_ref.shape[0] // CHUNK
    half = n_chunks // 2

    def at(group, pos, c):
        s = side if group is grp else 1 - side
        return (pos + s * (3 - 2 * pos)) * 2 + c

    barrier = pltpu.get_barrier_semaphore()

    def greet(i, _):
        to = (me + 1 + i) % 8
        pl.semaphore_signal(barrier, inc=1, device_id=(grp, to), device_id_type=MESH)
        return 0

    def greet_partner(i, _):
        pl.semaphore_signal(barrier, inc=1, device_id=(pgrp, i), device_id_type=MESH)
        return 0

    lax.fori_loop(0, 7, greet, 0)
    lax.fori_loop(0, 8, greet_partner, 0)
    local = pltpu.make_async_copy(own_ref, chip.at[core], chip_sems.at[0])
    local.start()
    pl.semaphore_wait(barrier, 15)

    def remote(src, dst, send, recv, group, to):
        return pltpu.make_async_remote_copy(
            src_ref=src, dst_ref=dst, send_sem=send, recv_sem=recv,
            device_id=(group, to), device_id_type=MESH,
        )

    def part(k):
        return pl.ds(pl.multiple_of(k * CHUNK, CHUNK), CHUNK)

    def to_held(k):
        return remote(own_ref.at[part(k)], held.at[part(k)], own_send.at[k], held_recv.at[k], grp, at(grp, w + 1, core))

    def to_other_partner(k):
        return remote(own_ref.at[part(k)], other.at[core, part(k)], own_send.at[k], other_recv.at[k], pgrp, me)

    def to_other_left(k):
        return remote(own_ref.at[part(k)], other.at[core, part(k)], own_send2.at[k], other_recv.at[k], grp, at(grp, 2, core))

    def pass_held(k):
        return remote(held.at[part(k)], passing.at[part(k)], held_send.at[k], passing_recv.at[k], pgrp, me)

    def pass_on(k):
        return remote(passing.at[part(k)], passing.at[part(k)], passing_send.at[k], passing_recv.at[k], grp, at(grp, w - 1, core))

    def share(k):
        return remote(other.at[core, part(k)], other.at[core, part(k)], other_send.at[k], sib_recv.at[k], grp, sib)

    def take_share(k):
        return remote(other.at[1 - core, part(k)], other.at[1 - core, part(k)], other_send.at[k], sib_recv.at[k], grp, sib)

    def issue(k):
        @pl.when(k < n_chunks)
        def _():
            @pl.when(w < 2)
            def _():
                to_held(k).start()

            @pl.when(w >= 2)
            def _():
                to_other_partner(k).start()

            @pl.when(w == 3)
            def _():
                to_other_left(k).start()

    def loop(lo, hi, body):
        def run(k, _):
            body(k)
            return 0
        lax.fori_loop(lo, hi, run, 0)

    swap = remote(own_ref, chip.at[core], sib_send.at[0], chip_sems.at[1], grp, sib)
    swapped = remote(own_ref, chip.at[1 - core], sib_send.at[0], chip_sems.at[1], grp, sib)
    swap.start()
    loop(0, AHEAD, issue)

    def req_copy(i):
        to = (me + 1 + i) % 8
        return remote(req_ref, reqs.at[me], req_send.at[i], req_recv.at[me], grp, to)

    loop(0, 7, lambda i: req_copy(i).start())

    def block(ref, lead, i):
        rows = pl.ds(pl.multiple_of(i * BLOCK, BLOCK), BLOCK)
        return ref[rows, :] if lead is None else ref[lead, rows, :]

    def inside(dev):
        def one(t):
            a, b = t % 2, t // 2
            s = scores_of(block(chip, dev, b), block(chip, core, a))
            r = lax.broadcasted_iota(jnp.int32, s.shape, 0)
            c = lax.broadcasted_iota(jnp.int32, s.shape, 1)
            same = jnp.logical_and(dev == core, a == b).astype(jnp.int32)
            limit = same * rows_ref[b] + (1 - same) * BLOCK
            drop = (r >= limit) | ((r - c) * same + (1 - same) == 0)
            best[dev + me - core, t] = jnp.max(jnp.where(drop, LOW, s), axis=0, keepdims=True)
        loop(0, 4, one)

    def cross(x, lead, i, ys, j0, n, stage):
        def one(t):
            yd, j = t % 2, j0 + t // 2
            s = scores_of(block(x, lead, i), block(ys, yd, j))
            out_y[stage, yd, i * 2 + j] = jnp.max(s, axis=0, keepdims=True)
            m = s[:, :128]
            for q in range(1, BLOCK // 128):
                m = jnp.maximum(m, s[:, q * 128:(q + 1) * 128])
            out_x[stage, yd, j * 2 + i] = jnp.max(m.T, axis=0, keepdims=True)
        loop(0, 2 * n, one)

    def x_back(stage, group, xid, yid, yd):
        return remote(out_x.at[stage, yd], best.at[yid], x_send.at[stage, yd], best_recv.at[yid], group, xid)

    def y_back(stage, group, xid, yid, yd):
        return remote(out_y.at[stage, yd], best.at[xid], y_send.at[stage, yd], best_recv.at[xid], group, yid)

    def chip_back(start):
        xid = at(grp, w - 1, core)
        ops = [x_back(0, grp, xid, at(grp, w, yd), yd) for yd in range(2)]
        ops.append(y_back(0, grp, xid, sib, 1 - core))
        for op in ops:
            op.start() if start else op.wait_send()
        if start:
            best[xid] = out_y[0, core]

    def pass_back(start):
        xid, pos = at(pgrp, 0, core), 3 - w
        for yd in range(2):
            yid = at(pgrp, pos, yd)
            for op in (x_back(1, pgrp, xid, yid, yd), y_back(1, pgrp, xid, yid, yd)):
                op.start() if start else op.wait_send()

    def far_back(start):
        xid = at(grp, 1, core)
        for yd in range(2):
            yid = at(grp, 3, yd)
            ops = (x_back(1, grp, xid, yid, yd), y_back(1, grp, xid, yid, yd), y_back(2, grp, me, yid, yd))
            for op in ops:
                op.start() if start else op.wait_send()
            if start:
                best[yid] = out_x[2, yd]

    def shares(lo, hi):
        loop(lo, hi, lambda k: take_share(k).wait_recv())

    def step0(s):
        issue(s + AHEAD)

        @pl.when(s < n_chunks)
        def _():
            to_other_partner(s).wait_recv()
            share(s).start()

        @pl.when(s >= 3)
        def _():
            pass_on(s - 3).wait_recv()

    def step1(s):
        issue(s + AHEAD)

        @pl.when(s < n_chunks)
        def _():
            to_held(s).wait_recv()
            pass_held(s).start()
            to_other_partner(s).wait_recv()
            share(s).start()

        @pl.when(s >= 2)
        def _():
            pass_on(s - 2).wait_recv()
            pass_on(s - 2).start()

    def step2(s):
        issue(s + AHEAD)

        @pl.when(s >= 1)
        def _():
            pass_held(s - 1).wait_recv()
            pass_on(s - 1).start()

        @pl.when(s < n_chunks)
        def _():
            to_other_left(s).wait_recv()
            share(s).start()
            to_held(s).wait_recv()

    local.wait()
    inside(core)
    swapped.wait_recv()

    @pl.when(w == 0)
    def _():
        inside(1 - core)
        loop(0, half + 4, step0)
        shares(0, half)
        cross(passing, None, 0, other, 0, 1, 1)
        loop(half + 4, n_chunks + 1, step0)
        shares(half, n_chunks)
        cross(passing, None, 0, other, 1, 1, 1)
        loop(n_chunks + 1, n_chunks + 3, step0)
        cross(passing, None, 1, other, 0, 2, 1)
        pass_back(True)
        loop(0, n_chunks, lambda k: to_held(k).wait_send())
        loop(0, n_chunks, lambda k: share(k).wait_send())
        pass_back(False)

    @pl.when(w == 1)
    def _():
        inside(1 - core)
        loop(0, half, step1)
        cross(held, None, 0, chip, 0, 2, 0)
        loop(half, half + 4, step1)
        shares(0, half)
        cross(passing, None, 0, other, 0, 1, 1)
        loop(half + 4, n_chunks, step1)
        cross(held, None, 1, chip, 0, 1, 0)
        loop(n_chunks, n_chunks + 1, step1)
        cross(held, None, 1, chip, 1, 1, 0)
        chip_back(True)
        loop(n_chunks + 1, n_chunks + 2, step1)
        shares(half, n_chunks)
        cross(passing, None, 0, other, 1, 1, 1)
        cross(passing, None, 1, other, 0, 2, 1)
        pass_back(True)
        loop(0, n_chunks, lambda k: to_held(k).wait_send())
        loop(0, n_chunks, lambda k: pass_held(k).wait_send())
        loop(0, n_chunks, lambda k: pass_on(k).wait_send())
        loop(0, n_chunks, lambda k: share(k).wait_send())
        chip_back(False)
        pass_back(False)

    @pl.when(w == 2)
    def _():
        inside(1 - core)
        loop(0, half, step2)
        cross(held, None, 0, chip, 0, 2, 0)
        loop(half, half + 2, step2)
        shares(0, half)
        cross(held, None, 0, other, 0, 1, 1)
        loop(half + 2, half + 4, step2)
        cross(own_ref, None, 0, other, 0, 1, 2)
        loop(half + 4, half + 6, step2)
        cross(own_ref, None, 1, other, 0, 1, 2)
        loop(half + 6, n_chunks, step2)
        cross(held, None, 1, chip, 0, 1, 0)
        loop(n_chunks, n_chunks + 1, step2)
        cross(held, None, 1, chip, 1, 1, 0)
        chip_back(True)
        shares(half, n_chunks)
        cross(held, None, 0, other, 1, 1, 1)
        cross(held, None, 1, other, 0, 2, 1)
        cross(own_ref, None, 0, other, 1, 1, 2)
        cross(own_ref, None, 1, other, 1, 1, 2)
        far_back(True)
        loop(0, n_chunks, lambda k: to_other_partner(k).wait_send())
        loop(0, n_chunks, lambda k: pass_on(k).wait_send())
        loop(0, n_chunks, lambda k: share(k).wait_send())
        chip_back(False)
        far_back(False)

    @pl.when(w == 3)
    def _():
        inside(1 - core)
        loop(AHEAD, n_chunks, issue)
        loop(0, n_chunks, lambda k: to_other_partner(k).wait_send())
        loop(0, n_chunks, lambda k: to_other_left(k).wait_send())

    swap.wait_send()
    loop(0, 7, lambda i: req_copy(i).wait_send())

    def req_arrived(i):
        o = (me + 1 + i) % 8
        remote(req_ref, reqs.at[o], req_send.at[i], req_recv.at[o], grp, o).wait_recv()

    loop(0, 7, req_arrived)

    def best_arrived(i):
        o = (me + 1 + i) % 8
        ow = o // 2 + side * (3 - 2 * (o // 2))
        here = (o == sib) | ((w == 1) & (ow == 0) & (o % 2 == core))
        here = here | ((w == 2) & (((ow == 1) & (o % 2 == core)) | (ow == 3)))

        @pl.when(jnp.logical_not(here))
        def _():
            remote(out_x.at[0, 0], best.at[o], x_send.at[0, 0], best_recv.at[o], grp, o).wait_recv()

    loop(0, 7, best_arrived)

    reqs[me] = req_ref[...]
    for a in range(2):
        def one(o, run):
            mine = req_ref[o]
            theirs = reqs[o, me]
            for b in range(2):
                listed = (mine == b) | (theirs == a)
                run = jnp.maximum(run, jnp.where(listed, best[o, b * 2 + a], LOW))
            return run
        out_ref[a] = lax.fori_loop(0, 8, one, jnp.full((1, BLOCK), LOW, jnp.float32))


def pooled(embedding, row_scale, block_rows, requests):
    blocks_here, width = block_rows.shape[0], embedding.shape[1]
    rows = blocks_here * BLOCK
    positions = jnp.arange(BLOCK, dtype=jnp.int32)
    live = positions[None, :] < block_rows[:, None]
    decoded = (embedding.astype(jnp.float32) * row_scale[:, None]).astype(jnp.bfloat16)
    decoded = decoded.reshape(blocks_here, BLOCK, width)
    decoded = jnp.where(live[:, :, None], decoded, decoded[:, :1, :]).reshape(rows, width)
    req = jnp.broadcast_to(requests.reshape(8, 1, 1), (8, 1, BLOCK))
    n = rows // CHUNK
    dma = pltpu.SemaphoreType.DMA
    highest = pl.pallas_call(
        kernel,
        out_shape=jax.ShapeDtypeStruct((blocks_here, 1, BLOCK), jnp.float32),
        in_specs=[pl.BlockSpec(memory_space=pltpu.SMEM)] + [pl.BlockSpec(memory_space=pltpu.VMEM)] * 2,
        out_specs=pl.BlockSpec(memory_space=pltpu.VMEM),
        scratch_shapes=[
            pltpu.VMEM((2, rows, width), jnp.bfloat16),
            pltpu.VMEM((rows, width), jnp.bfloat16),
            pltpu.VMEM((rows, width), jnp.bfloat16),
            pltpu.VMEM((2, rows, width), jnp.bfloat16),
            pltpu.VMEM((8, 4, 1, BLOCK), jnp.float32),
            pltpu.VMEM((3, 2, 4, 1, BLOCK), jnp.float32),
            pltpu.VMEM((3, 2, 4, 1, BLOCK), jnp.float32),
            pltpu.VMEM((8, 8, 1, BLOCK), jnp.int32),
        ] + [dma((n,))] * 5 + [dma((1,))] + [dma((n,))] * 4 + [
            dma((2,)), dma((8,)), dma((3, 2)), dma((3, 2)), dma((8,)), dma((8,)),
        ],
        compiler_params=pltpu.CompilerParams(
            collective_id=0, has_side_effects=True, vmem_limit_bytes=40 * 1024 * 1024
        ),
    )(block_rows, decoded, req)
    return jnp.where(live, highest[:, 0, :], jnp.float32(0.0)).reshape(-1)


def solution(mesh):
    small = mesh.shape["grp"] == 4 and mesh.shape["mem"] == 8
    return jax.shard_map(
        pooled if small else shards,
        mesh=mesh,
        in_specs=(
            P(("grp", "mem"), None),
            P(("grp", "mem")),
            P(("grp", "mem")),
            P(("grp", "mem"), None),
        ),
        out_specs=P(("grp", "mem")),
        check_vma=False,
    )
```

```python
import jax
import jax.numpy as jnp
from jax import lax
from jax.experimental import pallas as pl
from jax.experimental.pallas import tpu as pltpu
from jax.sharding import PartitionSpec as P

BLOCK = 512
SUB = 256
CHUNK = 64
AHEAD = 4
LOW = -1e30
MESH = pl.DeviceIdType.MESH


def shards(embedding, row_scale, block_rows, requests):
    members = lax.axis_size("mem")
    myself = lax.axis_index("mem")
    blocks_here = block_rows.shape[0]
    width = embedding.shape[1]
    decoded = (embedding.astype(jnp.float32) * row_scale[:, None]).astype(jnp.bfloat16)
    decoded = decoded.reshape(blocks_here, BLOCK, width)
    positions = jnp.arange(BLOCK, dtype=jnp.int32)
    local_live = positions[None, :] < block_rows[:, None]
    all_rows = lax.all_gather(block_rows, "mem", axis=0, tiled=True)
    wanted = lax.all_to_all(requests, "mem", split_axis=1, concat_axis=0, tiled=True)[:, 0]
    chosen = requests[0]
    local_ids = jnp.arange(blocks_here, dtype=jnp.int32)
    identity = positions[:, None] == positions[None, :]
    row_init = jnp.full((blocks_here, BLOCK), -1e30, dtype=jnp.float32)
    outgoing = jnp.take(decoded, wanted, axis=0)
    fetched = lax.all_to_all(outgoing, "mem", split_axis=0, concat_axis=0, tiled=True)
    owners = jnp.arange(members, dtype=jnp.int32)
    columns_live = positions[None, :] < all_rows[owners * blocks_here + chosen][:, None]
    own_block = jnp.where(owners == myself, chosen, -1)

    def visit(running, entries):
        partner, columns, own_index = entries
        scores = jnp.einsum("arc,sc->ars", decoded, partner, preferred_element_type=jnp.float32)
        diagonal = (local_ids[:, None, None] == own_index) & identity[None, :, :]
        allowed = columns[None, None, :] & jnp.logical_not(diagonal)
        masked = jnp.where(allowed, scores, jnp.float32(-1e30))
        running = jnp.maximum(running, jnp.max(masked, axis=2))
        column = jnp.max(jnp.where(local_live[:, :, None], masked, jnp.float32(-1e30)), axis=(0, 1))
        return (running, column)

    row_best, col_best = lax.scan(visit, row_init, (fetched, columns_live, own_block))
    returned = lax.all_to_all(col_best, "mem", split_axis=0, concat_axis=0, tiled=True)
    matches = wanted[None, :, None] == local_ids[:, None, None]
    incoming = jnp.max(jnp.where(matches, returned[None, :, :], jnp.float32(-1e30)), axis=1)
    highest = jnp.maximum(row_best, incoming)
    return jnp.where(local_live, highest, jnp.float32(0.0)).reshape(-1)


def scores_of(x, y):
    return lax.dot_general(x, y, (((1,), (1,)), ((), ())), preferred_element_type=jnp.float32)


def kernel(
    rows_ref, own_ref, req_ref, out_ref,
    chip, held, passing, other, best, out_x, out_y, reqs,
    own_send, own_send2, held_send, passing_send, other_send, sib_send,
    held_recv, passing_recv, other_recv, sib_recv, chip_sems,
    best_recv, x_send, y_send, req_send, req_recv,
):
    grp, me = lax.axis_index("grp"), lax.axis_index("mem")
    core, z = me % 2, me // 2
    side = grp % 2
    w = z + side * (3 - 2 * z)
    pgrp = grp + 1 - 2 * side
    sib = me + 1 - 2 * core
    n_chunks = own_ref.shape[0] // CHUNK
    per = SUB // CHUNK

    def at(group, pos, c):
        s = side if group is grp else 1 - side
        return (pos + s * (3 - 2 * pos)) * 2 + c

    barrier = pltpu.get_barrier_semaphore()

    def greet(i, _):
        to = (me + 1 + i) % 8
        pl.semaphore_signal(barrier, inc=1, device_id=(grp, to), device_id_type=MESH)
        return 0

    def greet_partner(i, _):
        pl.semaphore_signal(barrier, inc=1, device_id=(pgrp, i), device_id_type=MESH)
        return 0

    lax.fori_loop(0, 7, greet, 0)
    lax.fori_loop(0, 8, greet_partner, 0)
    local = pltpu.make_async_copy(own_ref, chip.at[core], chip_sems.at[0])
    local.start()
    pl.semaphore_wait(barrier, 15)

    def remote(src, dst, send, recv, group, to):
        return pltpu.make_async_remote_copy(
            src_ref=src, dst_ref=dst, send_sem=send, recv_sem=recv,
            device_id=(group, to), device_id_type=MESH,
        )

    def part(k):
        return pl.ds(pl.multiple_of(k * CHUNK, CHUNK), CHUNK)

    def to_held(k):
        return remote(own_ref.at[part(k)], held.at[part(k)], own_send.at[k], held_recv.at[k], grp, at(grp, w + 1, core))

    def to_other_partner(k):
        return remote(own_ref.at[part(k)], other.at[core, part(k)], own_send.at[k], other_recv.at[k], pgrp, me)

    def to_other_left(k):
        return remote(own_ref.at[part(k)], other.at[core, part(k)], own_send2.at[k], other_recv.at[k], grp, at(grp, 2, core))

    def pass_held(k):
        return remote(held.at[part(k)], passing.at[part(k)], held_send.at[k], passing_recv.at[k], pgrp, me)

    def pass_on(k):
        return remote(passing.at[part(k)], passing.at[part(k)], passing_send.at[k], passing_recv.at[k], grp, at(grp, w - 1, core))

    def share(k):
        return remote(other.at[core, part(k)], other.at[core, part(k)], other_send.at[k], sib_recv.at[k], grp, sib)

    def take_share(k):
        return remote(other.at[1 - core, part(k)], other.at[1 - core, part(k)], other_send.at[k], sib_recv.at[k], grp, sib)

    def issue(k):
        @pl.when(k < n_chunks)
        def _():
            @pl.when(w < 2)
            def _():
                to_held(k).start()

            @pl.when(w >= 2)
            def _():
                to_other_partner(k).start()

            @pl.when(w == 3)
            def _():
                to_other_left(k).start()

    def loop(lo, hi, body):
        def run(k, _):
            body(k)
            return 0
        lax.fori_loop(lo, hi, run, 0)

    swap = remote(own_ref, chip.at[core], sib_send.at[0], chip_sems.at[1], grp, sib)
    swapped = remote(own_ref, chip.at[1 - core], sib_send.at[0], chip_sems.at[1], grp, sib)
    swap.start()
    loop(0, AHEAD, issue)

    def req_copy(i):
        to = (me + 1 + i) % 8
        return remote(req_ref, reqs.at[me], req_send.at[i], req_recv.at[me], grp, to)

    loop(0, 7, lambda i: req_copy(i).start())

    def block(ref, lead, i):
        rows = pl.ds(pl.multiple_of(i * BLOCK, BLOCK), BLOCK)
        return ref[rows, :] if lead is None else ref[lead, rows, :]

    def inside(dev, t):
        a, b = t % 2, t // 2
        s = scores_of(block(chip, dev, b), block(chip, core, a))
        r = lax.broadcasted_iota(jnp.int32, s.shape, 0)
        c = lax.broadcasted_iota(jnp.int32, s.shape, 1)
        same = jnp.logical_and(dev == core, a == b).astype(jnp.int32)
        limit = same * rows_ref[b] + (1 - same) * BLOCK
        drop = (r >= limit) | ((r - c) * same + (1 - same) == 0)
        best[dev + me - core, t] = jnp.max(jnp.where(drop, LOW, s), axis=0, keepdims=True)

    def unit(x, xr, m, ys, yd, yr, n, stage):
        s = scores_of(x[pl.ds(pl.multiple_of(xr, SUB), m), :], ys[yd, pl.ds(pl.multiple_of(yr, SUB), n), :])
        i, j = xr // BLOCK, yr // BLOCK
        xl = pl.ds(pl.multiple_of(xr % BLOCK, SUB), m)
        yl = pl.ds(pl.multiple_of(yr % BLOCK, SUB), n)
        col = jnp.max(s, axis=0, keepdims=True)
        out_y[stage, yd, i * 2 + j, :, yl] = jnp.maximum(out_y[stage, yd, i * 2 + j, :, yl], col)
        part_max = s[:, :128]
        for q in range(1, n // 128):
            part_max = jnp.maximum(part_max, s[:, q * 128:(q + 1) * 128])
        row = jnp.max(part_max.T, axis=0, keepdims=True)
        out_x[stage, yd, j * 2 + i, :, xl] = jnp.maximum(out_x[stage, yd, j * 2 + i, :, xl], row)

    def new_rows(x, p, lo, hi):
        loop(lo, hi, lambda t: unit(x, p * SUB, SUB, chip, t % 2, (t // 2) * BLOCK, BLOCK, 0))

    def new_pairs(x, p):
        loop(0, 2 * (p + 1), lambda t: unit(x, p * SUB, SUB, other, t % 2, (t // 2) * SUB, SUB, 1))
        loop(0, 2 * p, lambda t: unit(x, (t // 2) * SUB, SUB, other, t % 2, p * SUB, SUB, 1))

    def x_back(stage, group, xid, yid, yd):
        return remote(out_x.at[stage, yd], best.at[yid], x_send.at[stage, yd], best_recv.at[yid], group, xid)

    def y_back(stage, group, xid, yid, yd):
        return remote(out_y.at[stage, yd], best.at[xid], y_send.at[stage, yd], best_recv.at[xid], group, yid)

    def chip_back(start):
        xid = at(grp, w - 1, core)
        ops = [x_back(0, grp, xid, at(grp, w, yd), yd) for yd in range(2)]
        ops.append(y_back(0, grp, xid, sib, 1 - core))
        for op in ops:
            op.start() if start else op.wait_send()
        if start:
            best[xid] = out_y[0, core]

    def pass_back(start):
        xid, pos = at(pgrp, 0, core), 3 - w
        for yd in range(2):
            yid = at(pgrp, pos, yd)
            for op in (x_back(1, pgrp, xid, yid, yd), y_back(1, pgrp, xid, yid, yd)):
                op.start() if start else op.wait_send()

    def far_back(start):
        xid = at(grp, 1, core)
        for yd in range(2):
            yid = at(grp, 3, yd)
            ops = (x_back(1, grp, xid, yid, yd), y_back(1, grp, xid, yid, yd), y_back(2, grp, me, yid, yd))
            for op in ops:
                op.start() if start else op.wait_send()
            if start:
                best[yid] = out_x[2, yd]

    def shares(lo, hi):
        loop(lo, hi, lambda k: take_share(k).wait_recv())

    def step0(s):
        issue(s + AHEAD)

        @pl.when(s < n_chunks)
        def _():
            to_other_partner(s).wait_recv()
            share(s).start()

        @pl.when((s >= 3) & (s < n_chunks + 3))
        def _():
            pass_on(s - 3).wait_recv()

    def step1(s):
        issue(s + AHEAD)

        @pl.when(s < n_chunks)
        def _():
            to_held(s).wait_recv()
            pass_held(s).start()
            to_other_partner(s).wait_recv()
            share(s).start()

        @pl.when((s >= 2) & (s < n_chunks + 2))
        def _():
            pass_on(s - 2).wait_recv()
            pass_on(s - 2).start()

    def step2(s):
        issue(s + AHEAD)

        @pl.when((s >= 1) & (s < n_chunks + 1))
        def _():
            pass_held(s - 1).wait_recv()
            pass_on(s - 1).start()

        @pl.when(s < n_chunks)
        def _():
            to_other_left(s).wait_recv()
            share(s).start()
            to_held(s).wait_recv()

    def work0(t, p):
        if t == 3:
            shares(p * per, (p + 1) * per)
            new_pairs(passing, p)

    def work1(t, p):
        if t < 2:
            new_rows(held, p, 2 * t, 2 * t + 2)
        elif t == 3:
            shares(p * per, (p + 1) * per)
            new_pairs(passing, p)

    def work2(t, p):
        if t == 0:
            new_rows(held, p, 0, 4)
        elif t < 3:
            if t == 1:
                shares(p * per, (p + 1) * per)
            loop(0, 2, lambda y: unit(own_ref, (t - 1) * BLOCK, BLOCK, other, y, p * SUB, SUB, 2))
        else:
            new_pairs(held, p)

    def phases(step, work):
        def phase(p):
            for t in range(per):
                step(p * per + t)

                @pl.when(p == 0)
                def _():
                    inside(core, t)
                    inside(1 - core, t)

                @pl.when(p > 0)
                def _():
                    work(t, p - 1)
        loop(0, n_chunks // per + 1, phase)

    out_x[...] = jnp.full(out_x.shape, LOW, out_x.dtype)
    out_y[...] = jnp.full(out_y.shape, LOW, out_y.dtype)
    local.wait()
    swapped.wait_recv()

    @pl.when(w == 0)
    def _():
        phases(step0, work0)
        pass_back(True)
        loop(0, n_chunks, lambda k: to_held(k).wait_send())
        loop(0, n_chunks, lambda k: share(k).wait_send())
        pass_back(False)

    @pl.when(w == 1)
    def _():
        phases(step1, work1)
        chip_back(True)
        pass_back(True)
        loop(0, n_chunks, lambda k: to_held(k).wait_send())
        loop(0, n_chunks, lambda k: pass_held(k).wait_send())
        loop(0, n_chunks, lambda k: pass_on(k).wait_send())
        loop(0, n_chunks, lambda k: share(k).wait_send())
        chip_back(False)
        pass_back(False)

    @pl.when(w == 2)
    def _():
        phases(step2, work2)
        chip_back(True)
        far_back(True)
        loop(0, n_chunks, lambda k: to_other_partner(k).wait_send())
        loop(0, n_chunks, lambda k: pass_on(k).wait_send())
        loop(0, n_chunks, lambda k: share(k).wait_send())
        chip_back(False)
        far_back(False)

    @pl.when(w == 3)
    def _():
        loop(AHEAD, n_chunks, issue)
        loop(0, 4, lambda t: inside(core, t))
        loop(0, 4, lambda t: inside(1 - core, t))
        loop(0, n_chunks, lambda k: to_other_partner(k).wait_send())
        loop(0, n_chunks, lambda k: to_other_left(k).wait_send())

    swap.wait_send()
    loop(0, 7, lambda i: req_copy(i).wait_send())

    def req_arrived(i):
        o = (me + 1 + i) % 8
        remote(req_ref, reqs.at[o], req_send.at[i], req_recv.at[o], grp, o).wait_recv()

    loop(0, 7, req_arrived)

    def best_arrived(i):
        o = (me + 1 + i) % 8
        ow = o // 2 + side * (3 - 2 * (o // 2))
        here = (o == sib) | ((w == 1) & (ow == 0) & (o % 2 == core))
        here = here | ((w == 2) & (((ow == 1) & (o % 2 == core)) | (ow == 3)))

        @pl.when(jnp.logical_not(here))
        def _():
            remote(out_x.at[0, 0], best.at[o], x_send.at[0, 0], best_recv.at[o], grp, o).wait_recv()

    loop(0, 7, best_arrived)

    reqs[me] = req_ref[...]
    for a in range(2):
        def one(o, run):
            mine = req_ref[o]
            theirs = reqs[o, me]
            for b in range(2):
                listed = (mine == b) | (theirs == a)
                run = jnp.maximum(run, jnp.where(listed, best[o, b * 2 + a], LOW))
            return run
        out_ref[a] = lax.fori_loop(0, 8, one, jnp.full((1, BLOCK), LOW, jnp.float32))


def pooled(embedding, row_scale, block_rows, requests):
    blocks_here, width = block_rows.shape[0], embedding.shape[1]
    rows = blocks_here * BLOCK
    positions = jnp.arange(BLOCK, dtype=jnp.int32)
    live = positions[None, :] < block_rows[:, None]
    decoded = (embedding.astype(jnp.float32) * row_scale[:, None]).astype(jnp.bfloat16)
    decoded = decoded.reshape(blocks_here, BLOCK, width)
    decoded = jnp.where(live[:, :, None], decoded, decoded[:, :1, :]).reshape(rows, width)
    req = jnp.broadcast_to(requests.reshape(8, 1, 1), (8, 1, BLOCK))
    n = rows // CHUNK
    dma = pltpu.SemaphoreType.DMA
    highest = pl.pallas_call(
        kernel,
        out_shape=jax.ShapeDtypeStruct((blocks_here, 1, BLOCK), jnp.float32),
        in_specs=[pl.BlockSpec(memory_space=pltpu.SMEM)] + [pl.BlockSpec(memory_space=pltpu.VMEM)] * 2,
        out_specs=pl.BlockSpec(memory_space=pltpu.VMEM),
        scratch_shapes=[
            pltpu.VMEM((2, rows, width), jnp.bfloat16),
            pltpu.VMEM((rows, width), jnp.bfloat16),
            pltpu.VMEM((rows, width), jnp.bfloat16),
            pltpu.VMEM((2, rows, width), jnp.bfloat16),
            pltpu.VMEM((8, 4, 1, BLOCK), jnp.float32),
            pltpu.VMEM((3, 2, 4, 1, BLOCK), jnp.float32),
            pltpu.VMEM((3, 2, 4, 1, BLOCK), jnp.float32),
            pltpu.VMEM((8, 8, 1, BLOCK), jnp.int32),
        ] + [dma((n,))] * 5 + [dma((1,))] + [dma((n,))] * 4 + [
            dma((2,)), dma((8,)), dma((3, 2)), dma((3, 2)), dma((8,)), dma((8,)),
        ],
        compiler_params=pltpu.CompilerParams(
            collective_id=0, has_side_effects=True, vmem_limit_bytes=40 * 1024 * 1024
        ),
    )(block_rows, decoded, req)
    return jnp.where(live, highest[:, 0, :], jnp.float32(0.0)).reshape(-1)


def solution(mesh):
    small = mesh.shape["grp"] == 4 and mesh.shape["mem"] == 8
    return jax.shard_map(
        pooled if small else shards,
        mesh=mesh,
        in_specs=(
            P(("grp", "mem"), None),
            P(("grp", "mem")),
            P(("grp", "mem")),
            P(("grp", "mem"), None),
        ),
        out_specs=P(("grp", "mem")),
        check_vma=False,
    )
```

```python
import jax
import jax.numpy as jnp
from jax import lax
from jax.experimental import pallas as pl
from jax.experimental.pallas import tpu as pltpu
from jax.sharding import PartitionSpec as P

BLOCK = 512
CHUNK = 64
AHEAD = 4
LOW = -1e30
MESH = pl.DeviceIdType.MESH


def shards(embedding, row_scale, block_rows, requests):
    members = lax.axis_size("mem")
    myself = lax.axis_index("mem")
    blocks_here = block_rows.shape[0]
    width = embedding.shape[1]
    decoded = (embedding.astype(jnp.float32) * row_scale[:, None]).astype(jnp.bfloat16)
    decoded = decoded.reshape(blocks_here, BLOCK, width)
    positions = jnp.arange(BLOCK, dtype=jnp.int32)
    local_live = positions[None, :] < block_rows[:, None]
    all_rows = lax.all_gather(block_rows, "mem", axis=0, tiled=True)
    wanted = lax.all_to_all(requests, "mem", split_axis=1, concat_axis=0, tiled=True)[:, 0]
    chosen = requests[0]
    local_ids = jnp.arange(blocks_here, dtype=jnp.int32)
    identity = positions[:, None] == positions[None, :]
    row_init = jnp.full((blocks_here, BLOCK), -1e30, dtype=jnp.float32)
    outgoing = jnp.take(decoded, wanted, axis=0)
    fetched = lax.all_to_all(outgoing, "mem", split_axis=0, concat_axis=0, tiled=True)
    owners = jnp.arange(members, dtype=jnp.int32)
    columns_live = positions[None, :] < all_rows[owners * blocks_here + chosen][:, None]
    own_block = jnp.where(owners == myself, chosen, -1)

    def visit(running, entries):
        partner, columns, own_index = entries
        scores = jnp.einsum("arc,sc->ars", decoded, partner, preferred_element_type=jnp.float32)
        diagonal = (local_ids[:, None, None] == own_index) & identity[None, :, :]
        allowed = columns[None, None, :] & jnp.logical_not(diagonal)
        masked = jnp.where(allowed, scores, jnp.float32(-1e30))
        running = jnp.maximum(running, jnp.max(masked, axis=2))
        column = jnp.max(jnp.where(local_live[:, :, None], masked, jnp.float32(-1e30)), axis=(0, 1))
        return (running, column)

    row_best, col_best = lax.scan(visit, row_init, (fetched, columns_live, own_block))
    returned = lax.all_to_all(col_best, "mem", split_axis=0, concat_axis=0, tiled=True)
    matches = wanted[None, :, None] == local_ids[:, None, None]
    incoming = jnp.max(jnp.where(matches, returned[None, :, :], jnp.float32(-1e30)), axis=1)
    highest = jnp.maximum(row_best, incoming)
    return jnp.where(local_live, highest, jnp.float32(0.0)).reshape(-1)


def scores_of(x, y):
    return lax.dot_general(x, y, (((1,), (1,)), ((), ())), preferred_element_type=jnp.float32)


def kernel(
    rows_ref, own_ref, req_ref, out_ref,
    chip, held, passing, other, best, out_x, out_y, reqs,
    own_send, own_send2, held_send, passing_send, other_send, sib_send,
    held_recv, passing_recv, other_recv, sib_recv, chip_sems,
    best_recv, x_send, y_send, req_send, req_recv,
):
    grp, me = lax.axis_index("grp"), lax.axis_index("mem")
    core, z = me % 2, me // 2
    side = grp % 2
    w = z + side * (3 - 2 * z)
    pgrp = grp + 1 - 2 * side
    sib = me + 1 - 2 * core
    n_chunks = own_ref.shape[0] // CHUNK
    half = n_chunks // 2

    def at(group, pos, c):
        s = side if group is grp else 1 - side
        return (pos + s * (3 - 2 * pos)) * 2 + c

    barrier = pltpu.get_barrier_semaphore()

    def greet(i, _):
        to = (me + 1 + i) % 8
        pl.semaphore_signal(barrier, inc=1, device_id=(grp, to), device_id_type=MESH)
        return 0

    def greet_partner(i, _):
        pl.semaphore_signal(barrier, inc=1, device_id=(pgrp, i), device_id_type=MESH)
        return 0

    lax.fori_loop(0, 7, greet, 0)
    lax.fori_loop(0, 8, greet_partner, 0)
    local = pltpu.make_async_copy(own_ref, chip.at[core], chip_sems.at[0])
    local.start()
    pl.semaphore_wait(barrier, 15)

    def remote(src, dst, send, recv, group, to):
        return pltpu.make_async_remote_copy(
            src_ref=src, dst_ref=dst, send_sem=send, recv_sem=recv,
            device_id=(group, to), device_id_type=MESH,
        )

    def part(k):
        return pl.ds(pl.multiple_of(k * CHUNK, CHUNK), CHUNK)

    def to_held(k):
        return remote(own_ref.at[part(k)], held.at[part(k)], own_send.at[k], held_recv.at[k], grp, at(grp, w + 1, core))

    def to_other_partner(k):
        return remote(own_ref.at[part(k)], other.at[core, part(k)], own_send.at[k], other_recv.at[k], pgrp, me)

    def to_other_left(k):
        return remote(own_ref.at[part(k)], other.at[core, part(k)], own_send2.at[k], other_recv.at[k], grp, at(grp, 2, core))

    def pass_held(k):
        return remote(held.at[part(k)], passing.at[part(k)], held_send.at[k], passing_recv.at[k], pgrp, me)

    def hop(k):
        return remote(held.at[part(k)], held.at[part(k)], held_send.at[k], held_recv.at[k], grp, at(grp, 3, core))

    def pass_on(k):
        return remote(passing.at[part(k)], passing.at[part(k)], passing_send.at[k], passing_recv.at[k], grp, at(grp, w - 1, core))

    def share(k):
        return remote(other.at[core, part(k)], other.at[core, part(k)], other_send.at[k], sib_recv.at[k], grp, sib)

    def take_share(k):
        return remote(other.at[1 - core, part(k)], other.at[1 - core, part(k)], other_send.at[k], sib_recv.at[k], grp, sib)

    def issue(k):
        @pl.when(k < n_chunks)
        def _():
            @pl.when(w < 2)
            def _():
                to_held(k).start()

            @pl.when(w >= 2)
            def _():
                to_other_partner(k).start()

            @pl.when(w == 3)
            def _():
                to_other_left(k).start()

    def loop(lo, hi, body):
        def run(k, _):
            body(k)
            return 0
        lax.fori_loop(lo, hi, run, 0)

    swap = remote(own_ref, chip.at[core], sib_send.at[0], chip_sems.at[1], grp, sib)
    swapped = remote(own_ref, chip.at[1 - core], sib_send.at[0], chip_sems.at[1], grp, sib)
    swap.start()
    loop(0, AHEAD, issue)

    def req_copy(i):
        to = (me + 1 + i) % 8
        return remote(req_ref, reqs.at[me], req_send.at[i], req_recv.at[me], grp, to)

    loop(0, 7, lambda i: req_copy(i).start())

    def block(ref, lead, i):
        rows = pl.ds(pl.multiple_of(i * BLOCK, BLOCK), BLOCK)
        return ref[rows, :] if lead is None else ref[lead, rows, :]

    def inside(dev):
        def one(t):
            a, b = t % 2, t // 2
            s = scores_of(block(chip, dev, b), block(chip, core, a))
            r = lax.broadcasted_iota(jnp.int32, s.shape, 0)
            c = lax.broadcasted_iota(jnp.int32, s.shape, 1)
            same = jnp.logical_and(dev == core, a == b).astype(jnp.int32)
            limit = same * rows_ref[b] + (1 - same) * BLOCK
            drop = (r >= limit) | ((r - c) * same + (1 - same) == 0)
            best[dev + me - core, t] = jnp.max(jnp.where(drop, LOW, s), axis=0, keepdims=True)
        loop(0, 4, one)

    def cross(x, lead, i, ys, j0, n, stage):
        def one(t):
            yd, j = t % 2, j0 + t // 2
            s = scores_of(block(x, lead, i), block(ys, yd, j))
            out_y[stage, yd, i * 2 + j] = jnp.max(s, axis=0, keepdims=True)
            m = s[:, :128]
            for q in range(1, BLOCK // 128):
                m = jnp.maximum(m, s[:, q * 128:(q + 1) * 128])
            out_x[stage, yd, j * 2 + i] = jnp.max(m.T, axis=0, keepdims=True)
        loop(0, 2 * n, one)

    def x_back(stage, group, xid, yid, yd):
        return remote(out_x.at[stage, yd], best.at[yid], x_send.at[stage, yd], best_recv.at[yid], group, xid)

    def y_back(stage, group, xid, yid, yd):
        return remote(out_y.at[stage, yd], best.at[xid], y_send.at[stage, yd], best_recv.at[xid], group, yid)

    def chip_back(start, pos):
        xid = at(grp, pos, core)
        ops = [x_back(0, grp, xid, at(grp, w, yd), yd) for yd in range(2)]
        ops.append(y_back(0, grp, xid, sib, 1 - core))
        for op in ops:
            op.start() if start else op.wait_send()
        if start:
            best[xid] = out_y[0, core]

    def pass_back(start):
        xid, pos = at(pgrp, 0, core), 3 - w
        for yd in range(2):
            yid = at(pgrp, pos, yd)
            for op in (x_back(1, pgrp, xid, yid, yd), y_back(1, pgrp, xid, yid, yd)):
                op.start() if start else op.wait_send()

    def far_back(start):
        for yd in range(2):
            yid = at(grp, 3, yd)
            op = y_back(2, grp, me, yid, yd)
            op.start() if start else op.wait_send()
            if start:
                best[yid] = out_x[2, yd]

    def shares(lo, hi):
        loop(lo, hi, lambda k: take_share(k).wait_recv())

    def step0(s):
        issue(s + AHEAD)

        @pl.when(s < n_chunks)
        def _():
            to_other_partner(s).wait_recv()
            share(s).start()

        @pl.when(s >= 3)
        def _():
            pass_on(s - 3).wait_recv()

    def step1(s):
        issue(s + AHEAD)

        @pl.when(s < n_chunks)
        def _():
            to_held(s).wait_recv()
            pass_held(s).start()
            to_other_partner(s).wait_recv()
            share(s).start()

        @pl.when(s >= 2)
        def _():
            pass_on(s - 2).wait_recv()
            pass_on(s - 2).start()

    def step2(s):
        issue(s + AHEAD)

        @pl.when(s >= 1)
        def _():
            pass_held(s - 1).wait_recv()
            pass_on(s - 1).start()

        @pl.when(s < n_chunks)
        def _():
            to_other_left(s).wait_recv()
            share(s).start()
            to_held(s).wait_recv()
            hop(s).start()

    def step3(s):
        issue(s + AHEAD)
        hop(s).wait_recv()

    local.wait()
    inside(core)
    swapped.wait_recv()

    @pl.when(w == 0)
    def _():
        loop(0, half, step0)
        inside(1 - core)
        loop(half, half + 4, step0)
        shares(0, half)
        cross(passing, None, 0, other, 0, 1, 1)
        loop(half + 4, n_chunks + 1, step0)
        shares(half, n_chunks)
        cross(passing, None, 0, other, 1, 1, 1)
        loop(n_chunks + 1, n_chunks + 3, step0)
        cross(passing, None, 1, other, 0, 2, 1)
        pass_back(True)
        loop(0, n_chunks, lambda k: to_held(k).wait_send())
        loop(0, n_chunks, lambda k: share(k).wait_send())
        pass_back(False)

    @pl.when(w == 1)
    def _():
        loop(0, half, step1)
        cross(held, None, 0, chip, 0, 2, 0)
        loop(half, half + 4, step1)
        shares(0, half)
        cross(passing, None, 0, other, 0, 1, 1)
        loop(half + 4, n_chunks + 2, step1)
        shares(half, n_chunks)
        cross(passing, None, 0, other, 1, 1, 1)
        cross(passing, None, 1, other, 0, 2, 1)
        pass_back(True)
        cross(held, None, 1, chip, 0, 2, 0)
        chip_back(True, 0)
        inside(1 - core)
        loop(0, n_chunks, lambda k: to_held(k).wait_send())
        loop(0, n_chunks, lambda k: pass_held(k).wait_send())
        loop(0, n_chunks, lambda k: pass_on(k).wait_send())
        loop(0, n_chunks, lambda k: share(k).wait_send())
        chip_back(False, 0)
        pass_back(False)

    @pl.when(w == 2)
    def _():
        loop(0, half, step2)
        cross(held, None, 0, chip, 0, 2, 0)
        loop(half, half + 4, step2)
        shares(0, half)
        cross(own_ref, None, 0, other, 0, 1, 2)
        loop(half + 4, n_chunks + 1, step2)
        cross(held, None, 1, chip, 0, 2, 0)
        chip_back(True, 1)
        cross(own_ref, None, 1, other, 0, 1, 2)
        shares(half, n_chunks)
        cross(own_ref, None, 0, other, 1, 1, 2)
        cross(own_ref, None, 1, other, 1, 1, 2)
        far_back(True)
        inside(1 - core)
        loop(0, n_chunks, lambda k: to_other_partner(k).wait_send())
        loop(0, n_chunks, lambda k: hop(k).wait_send())
        loop(0, n_chunks, lambda k: pass_on(k).wait_send())
        loop(0, n_chunks, lambda k: share(k).wait_send())
        chip_back(False, 1)
        far_back(False)

    @pl.when(w == 3)
    def _():
        loop(0, half, step3)
        inside(1 - core)
        cross(held, None, 0, chip, 0, 2, 0)
        loop(half, n_chunks, step3)
        cross(held, None, 1, chip, 0, 2, 0)
        chip_back(True, 1)
        loop(0, n_chunks, lambda k: to_other_partner(k).wait_send())
        loop(0, n_chunks, lambda k: to_other_left(k).wait_send())
        chip_back(False, 1)

    swap.wait_send()
    loop(0, 7, lambda i: req_copy(i).wait_send())

    def req_arrived(i):
        o = (me + 1 + i) % 8
        remote(req_ref, reqs.at[o], req_send.at[i], req_recv.at[o], grp, o).wait_recv()

    loop(0, 7, req_arrived)

    def best_arrived(i):
        o = (me + 1 + i) % 8
        ow = o // 2 + side * (3 - 2 * (o // 2))
        here = (o == sib) | ((w == 1) & (ow == 0) & (o % 2 == core))
        here = here | ((w == 3) & (ow == 1) & (o % 2 == core))
        here = here | ((w == 2) & (((ow == 1) & (o % 2 == core)) | (ow == 3)))

        @pl.when(jnp.logical_not(here))
        def _():
            remote(out_x.at[0, 0], best.at[o], x_send.at[0, 0], best_recv.at[o], grp, o).wait_recv()

    loop(0, 7, best_arrived)

    reqs[me] = req_ref[...]
    for a in range(2):
        def one(o, run):
            mine = req_ref[o]
            theirs = reqs[o, me]
            for b in range(2):
                listed = (mine == b) | (theirs == a)
                run = jnp.maximum(run, jnp.where(listed, best[o, b * 2 + a], LOW))
            return run
        out_ref[a] = lax.fori_loop(0, 8, one, jnp.full((1, BLOCK), LOW, jnp.float32))


def pooled(embedding, row_scale, block_rows, requests):
    blocks_here, width = block_rows.shape[0], embedding.shape[1]
    rows = blocks_here * BLOCK
    positions = jnp.arange(BLOCK, dtype=jnp.int32)
    live = positions[None, :] < block_rows[:, None]
    decoded = (embedding.astype(jnp.float32) * row_scale[:, None]).astype(jnp.bfloat16)
    decoded = decoded.reshape(blocks_here, BLOCK, width)
    decoded = jnp.where(live[:, :, None], decoded, decoded[:, :1, :]).reshape(rows, width)
    req = jnp.broadcast_to(requests.reshape(8, 1, 1), (8, 1, BLOCK))
    n = rows // CHUNK
    dma = pltpu.SemaphoreType.DMA
    highest = pl.pallas_call(
        kernel,
        out_shape=jax.ShapeDtypeStruct((blocks_here, 1, BLOCK), jnp.float32),
        in_specs=[pl.BlockSpec(memory_space=pltpu.SMEM)] + [pl.BlockSpec(memory_space=pltpu.VMEM)] * 2,
        out_specs=pl.BlockSpec(memory_space=pltpu.VMEM),
        scratch_shapes=[
            pltpu.VMEM((2, rows, width), jnp.bfloat16),
            pltpu.VMEM((rows, width), jnp.bfloat16),
            pltpu.VMEM((rows, width), jnp.bfloat16),
            pltpu.VMEM((2, rows, width), jnp.bfloat16),
            pltpu.VMEM((8, 4, 1, BLOCK), jnp.float32),
            pltpu.VMEM((3, 2, 4, 1, BLOCK), jnp.float32),
            pltpu.VMEM((3, 2, 4, 1, BLOCK), jnp.float32),
            pltpu.VMEM((8, 8, 1, BLOCK), jnp.int32),
        ] + [dma((n,))] * 5 + [dma((1,))] + [dma((n,))] * 4 + [
            dma((2,)), dma((8,)), dma((3, 2)), dma((3, 2)), dma((8,)), dma((8,)),
        ],
        compiler_params=pltpu.CompilerParams(
            collective_id=0, has_side_effects=True, vmem_limit_bytes=40 * 1024 * 1024
        ),
    )(block_rows, decoded, req)
    return jnp.where(live, highest[:, 0, :], jnp.float32(0.0)).reshape(-1)


def solution(mesh):
    small = mesh.shape["grp"] == 4 and mesh.shape["mem"] == 8
    return jax.shard_map(
        pooled if small else shards,
        mesh=mesh,
        in_specs=(
            P(("grp", "mem"), None),
            P(("grp", "mem")),
            P(("grp", "mem")),
            P(("grp", "mem"), None),
        ),
        out_specs=P(("grp", "mem")),
        check_vma=False,
    )
```
